512 devices in a mesh: gx: 16 (over z), gy: 16 (over x, y), gz: 2 (over core).
Axes of the slice: x: 4, y: 4, z: 16, core: 2. Of those that a mesh axis runs over, the one named last changes fastest.
Arguments:
- moment: bfloat16 [1024, 1024, 1024], P('gx', 'gy', 'gz'), may hold values from -0.625 to 0.625
- factor_start: bfloat16 [1024, 128], replicated, may hold values from -6 to 6
Outputs:
- factor_out: float32 [1024, 128], P('gx')
The draws below stay inside these ranges and needn't reach their ends.
All inputs are finite; a program needn't handle non-finite values.
Results may differ from the reference program's by a relative error of at most 0.0005.
Values may be sent and summed in bfloat16 or wider, within the bound.
No kernel may reach another device: no remote copies, remote signals or barrier semaphores. Data moves between devices by JAX's collectives and lax.ppermute only.
A program may use at most 64 MiB of HBM per device.

```python
import jax
import jax.numpy as jnp
from jax import lax

N = 1024
R = 128
ITERS = 1
N_GZ = 2


def draw_moment(key, part):
    key = jax.random.fold_in(key, 11)
    noise_key, shared_key, block_key = jax.random.split(key, 3)
    position = jnp.arange(N, dtype=jnp.float32) / (N - 1)
    row_block = jnp.arange(N, dtype=jnp.int32) // 16
    block_draw = jax.random.uniform(block_key, (N // 16,), jnp.float32, 0.0, 1.0)
    shared = jnp.clip(jax.random.normal(shared_key, (N, N), jnp.float32), -2.0833, 2.0833)
    base = jnp.clip(jax.random.normal(noise_key, (N, N, N), jnp.float32), -6.0, 6.0)
    rise = jnp.exp(jnp.log(3.2) * position)
    jitter = jnp.exp(jnp.log(0.55) * block_draw)
    row_scale = rise * jitter[row_block]
    values = (0.7 * base + 0.3 * shared[None, :, :]) * N ** (-0.5) * row_scale[:, None, None]
    return values.astype(jnp.bfloat16)


def gaussian(rng, shape, width, most, held_as=jnp.bfloat16):
    array = jax.random.normal(rng, shape, jnp.float32) * width
    return jnp.minimum(jnp.maximum(array, -most), most).astype(held_as)


def setup_inputs(seed: int = 0) -> dict:
    key_of = jax.random.split(jax.random.key(seed), 3)
    return {
        "moment": draw_moment(jax.random.fold_in(key_of[2], 71), 0),
        "factor_start": gaussian(key_of[1], (N, R), 1.0, 6.0),
    }


def reference(moment, factor_start):
    kblk = N // N_GZ
    scale_n = 1.0 / N ** 0.5
    factor = factor_start
    blocks = moment.reshape(N // 32, 32, N, N)
    result = None
    for sweep in range(ITERS):

        def mode_block(block):
            acc = jnp.zeros((block.shape[0], N, R), jnp.float32)
            for part in range(N_GZ):
                piece = jnp.einsum('ijk,kb->ijb', block[:, :, part * kblk:(part + 1) * kblk].astype(jnp.float32), factor[part * kblk:(part + 1) * kblk].astype(jnp.float32))
                piece = lax.optimization_barrier(piece.astype(jnp.bfloat16))
                acc = acc + piece.astype(jnp.float32)
            ytens = acc.astype(jnp.bfloat16)
            ztens = jnp.einsum('ijb,ja->iba', ytens.astype(jnp.float32), factor.astype(jnp.float32)) * scale_n
            return ztens.astype(jnp.bfloat16)
        zfull = lax.map(mode_block, blocks).reshape(N, R, R)
        cgram = jnp.einsum('iba,ir->bar', zfull.astype(jnp.float32), factor.astype(jnp.float32)) * scale_n
        cgram = cgram.astype(jnp.bfloat16)
        vnew = jnp.einsum('iba,bar->ir', zfull.astype(jnp.float32), cgram.astype(jnp.float32)) / R
        total = jnp.sum(vnew * vnew)
        result = vnew * lax.rsqrt(total / (N * R) + 1e-06)
        factor = result.astype(jnp.bfloat16)
    return result
```

```python
import jax
import jax.numpy as jnp
from jax import lax
from jax.experimental import pallas as pl
from jax.experimental.pallas import tpu as pltpu
from jax.sharding import PartitionSpec as P

F32 = jnp.float32
BF16 = jnp.bfloat16
MIB = 1 << 20
VMEM = pl.BlockSpec(memory_space=pltpu.VMEM)
SMEM = pl.BlockSpec(memory_space=pltpu.SMEM)


def params(mib):
    return pltpu.CompilerParams(vmem_limit_bytes=mib * MIB)


PAIRS = 8


def y_kernel(half_ref, lo_ref, hi_ref, u_ref, out_ref, ut_ref):
    del half_ref

    @pl.when(pl.program_id(0) == 0)
    def _():
        ut_ref[...] = u_ref[...].T

    ut = ut_ref[...]

    def one(p):
        rows = jnp.concatenate([lo_ref[p], hi_ref[p]], axis=0)
        y = lax.dot_general(ut, rows, (((1,), (1,)), ((), ())), preferred_element_type=F32)
        return y.reshape(16, 8, 128)

    for p in range(0, PAIRS, 2):
        out_ref[:, 8 * p : 8 * p + 16, :] = jnp.concatenate([one(p), one(p + 1)], axis=1).astype(BF16)


def y_half(half, core, moment, factor):
    steps = 16 // PAIRS
    return pl.pallas_call(
        y_kernel,
        out_shape=jax.ShapeDtypeStruct((16, 128, 128), BF16),
        grid_spec=pltpu.PrefetchScalarGridSpec(
            num_scalar_prefetch=1,
            grid=(steps,),
            in_specs=[
                pl.BlockSpec((PAIRS, 64, 512), lambda t, s: (s[0] * 2 * steps + t, 0, 0)),
                pl.BlockSpec((PAIRS, 64, 512), lambda t, s: (s[0] * 2 * steps + steps + t, 0, 0)),
                pl.BlockSpec((512, 128), lambda t, s: (s[1], 0)),
            ],
            out_specs=pl.BlockSpec((16, 8 * PAIRS, 128), lambda t, s: (0, t, 0)),
            scratch_shapes=[pltpu.VMEM((128, 512), BF16)],
        ),
        compiler_params=params(56),
        name="y_half",
    )(jnp.stack([half, core]).astype(jnp.int32), moment, moment, factor)


def z_kernel(y_ref, u_ref, out_ref, w_ref, z_ref):
    w_ref[...] = jnp.zeros(w_ref.shape, BF16)
    for s in range(16):
        block = u_ref[64 * s : 64 * s + 64, :]
        w_ref[128 * s : 128 * s + 64, 0:128] = block
        w_ref[128 * s + 64 : 128 * s + 128, 128:256] = block
    lhs = jnp.concatenate([y_ref[s] for s in range(16)], axis=1)
    z = jnp.dot(lhs, w_ref[...], preferred_element_type=F32) * (1.0 / 32.0)
    z_ref[0] = z[:, 0:128]
    z_ref[1] = z[:, 128:256]
    for b in range(8):
        zb = [z_ref[i2, pl.ds(b, 16, stride=8), :] for i2 in range(2)]
        parts = []
        for q in range(4):
            cut = [
                zb[i2][8 * iph : 8 * iph + 8, 32 * q : 32 * q + 32]
                for i2 in range(2)
                for iph in range(2)
            ]
            parts.append(jnp.concatenate(cut, axis=1))
        out_ref[32 * b : 32 * b + 32, :] = jnp.concatenate(parts, axis=0).astype(BF16)


def v_kernel(z_ref, u_ref, out_ref, w_ref, v_ref):
    zt = z_ref[...]
    u = u_ref[...].astype(F32).reshape(32, 4, 8, 128)
    uw = jnp.concatenate([u[:, s].reshape(256, 128) for s in range(4)], axis=1).astype(BF16)
    full = lax.dot_general(zt, uw, (((0,), (0,)), ((), ())), preferred_element_type=F32)
    c = full[0:32, 0:128]
    for s in range(1, 4):
        c = c + full[32 * s : 32 * s + 32, 128 * s : 128 * s + 128]
    c = (c * (1.0 / 32.0)).astype(BF16)
    w_ref[...] = jnp.zeros(w_ref.shape, BF16)
    for s in range(4):
        w_ref[32 * s : 32 * s + 32, 128 * s : 128 * s + 128] = c
    v = jnp.dot(zt, w_ref[...], preferred_element_type=F32)
    for s in range(4):
        v_ref[s] = v[:, 128 * s : 128 * s + 128]
        for row in range(8):
            out_ref[8 * s + row] = v_ref[s, pl.ds(row, 32, stride=8), :]


def sum_kernel(in_ref, out_ref):
    total = jnp.sum(in_ref[...], axis=0)
    out_ref[...] = jnp.broadcast_to(total[None], out_ref.shape)


def rows_kernel(idx_ref, in_ref, out_ref, v_ref):
    v = jnp.sum(in_ref[...], axis=0)
    v_ref[...] = v
    squares = jnp.sum(v * v, axis=0, keepdims=True)
    own = v_ref[pl.ds(2 * idx_ref[0], 2), :]
    block = jnp.concatenate([own, squares, jnp.zeros((5, 128), F32)], axis=0)
    out_ref[...] = jnp.broadcast_to(block[None], out_ref.shape)


def final_kernel(in_ref, out_ref):
    total = jnp.sum(in_ref[pl.ds(2, 32, stride=8), :]) * (1.0 / (128.0 * 128.0))
    scale = lax.rsqrt(total / (1024 * 128) + 1e-06) * (1.0 / 128.0)
    out_ref[0:32, :] = in_ref[pl.ds(0, 32, stride=8), :] * scale
    out_ref[32:64, :] = in_ref[pl.ds(1, 32, stride=8), :] * scale


def call(kernel, out, specs, scratch, mib, name):
    return pl.pallas_call(
        kernel,
        out_shape=jax.ShapeDtypeStruct(*out),
        in_specs=specs,
        out_specs=VMEM,
        scratch_shapes=scratch,
        compiler_params=params(mib),
        name=name,
    )


def local(moment, factor):
    plane = ("gy", "gz")
    idx_x = lax.axis_index("gx").astype(jnp.int32).reshape(1)
    core = lax.axis_index("gz")
    there = y_half(1 - core, core, moment, factor)
    came = lax.ppermute(there, "gz", [(0, 1), (1, 0)])
    here = y_half(core, core, moment, factor)
    y = (here.astype(F32) + came.astype(F32)).astype(BF16)
    y = lax.all_to_all(y, "gy", 0, 0, tiled=True)
    z = call(
        z_kernel,
        ((256, 128), BF16),
        [VMEM, VMEM],
        [pltpu.VMEM((2048, 256), BF16), pltpu.VMEM((2, 128, 128), F32)],
        8,
        "z_block",
    )(y, factor)
    z = lax.all_to_all(z.reshape(32, 8, 128), ("gx", "gz"), 0, 0, tiled=True)
    v = call(
        v_kernel,
        ((32, 32, 128), F32),
        [VMEM, VMEM],
        [pltpu.VMEM((128, 512), BF16), pltpu.VMEM((4, 256, 128), F32)],
        8,
        "v_part",
    )(z.reshape(256, 128), factor)
    v = lax.all_to_all(v, plane, 0, 0, tiled=True)
    v = call(sum_kernel, ((16, 32, 128), F32), [VMEM], [], 8, "v_sum_plane")(v)
    v = lax.all_to_all(v, "gx", 0, 0, tiled=True)
    v = call(
        rows_kernel, ((32, 8, 128), F32), [SMEM, VMEM], [pltpu.VMEM((32, 128), F32)], 8, "v_rows"
    )(idx_x, v)
    v = lax.all_to_all(v, plane, 0, 0, tiled=True)
    return call(final_kernel, ((64, 128), F32), [VMEM], [], 8, "scaled")(v.reshape(256, 128))


def solution(mesh):
    in_specs = (P("gx", "gy", "gz"), P())
    out_specs = P("gx", None)
    return jax.shard_map(local, mesh=mesh, in_specs=in_specs, out_specs=out_specs, check_vma=False)
```

```python
import jax
import jax.numpy as jnp
from jax import lax
from jax.experimental import pallas as pl
from jax.experimental.pallas import tpu as pltpu
from jax.sharding import PartitionSpec as P

F32 = jnp.float32
BF16 = jnp.bfloat16
MIB = 1 << 20
VMEM = pl.BlockSpec(memory_space=pltpu.VMEM)
ANY = pl.BlockSpec(memory_space=pl.ANY)
SMEM = pl.BlockSpec(memory_space=pltpu.SMEM)


def params(mib):
    return pltpu.CompilerParams(vmem_limit_bytes=mib * MIB)


def y_store(ut, rows, first, out_ref):
    y = lax.dot_general(ut, rows, (((1,), (1,)), ((), ())), preferred_element_type=F32)
    parts = [y[:, n : n + 128].reshape(16, 8, 128) for n in range(0, y.shape[1], 128)]
    out_ref[:, 8 * first : 8 * (first + len(parts)), :] = jnp.concatenate(parts, axis=1).astype(BF16)


CHUNK = 8
CHUNKS = 16 // CHUNK
DOT = 2
HALF = (CHUNKS, 2, CHUNK, 64, 512)


def y_copies(half, m_ref, buf, sem):
    copies = []
    for t in range(CHUNKS):
        for h in range(2):
            block = m_ref.at[pl.ds(32 * half + 16 * h + CHUNK * t, CHUNK)]
            copies.append(pltpu.make_async_copy(block, buf.at[t, h], sem.at[t, h]))
            copies[-1].start()
    return copies


def y_chunk(t, ut, buf, out_ref):
    for p in range(0, CHUNK, DOT):
        rows = jnp.concatenate([buf[t, h, p + n] for n in range(DOT) for h in range(2)], axis=0)
        y_store(ut, rows, CHUNK * t + p, out_ref)


def y_there_kernel(idx_ref, m_ref, u_ref, out_ref, ut_ref, mine_ref, buf, ubuf, sem, mine_sem, usem):
    core = lax.rem(idx_ref[0], 2)
    ucopy = pltpu.make_async_copy(u_ref.at[pl.ds(512 * core, 512)], ubuf, usem)
    ucopy.start()
    copies = y_copies(1 - core, m_ref, buf, sem)
    mine = y_copies(core, m_ref, mine_ref, mine_sem)
    ucopy.wait()
    ut_ref[...] = ubuf[...].T
    for t in range(CHUNKS):
        copies[2 * t].wait()
        copies[2 * t + 1].wait()
        y_chunk(t, ut_ref[...], buf, out_ref)
    for copy in mine:
        copy.wait()


def y_here_kernel(m_ref, ut_ref, out_ref):
    for t in range(CHUNKS):
        y_chunk(t, ut_ref[...], m_ref, out_ref)


def y_there(idx, moment, factor):
    return pl.pallas_call(
        y_there_kernel,
        out_shape=[
            jax.ShapeDtypeStruct((16, 128, 128), BF16),
            jax.ShapeDtypeStruct((128, 512), BF16),
            jax.ShapeDtypeStruct(HALF, BF16),
        ],
        in_specs=[SMEM, ANY, ANY],
        out_specs=[VMEM, VMEM, VMEM],
        scratch_shapes=[
            pltpu.VMEM(HALF, BF16),
            pltpu.VMEM((512, 128), BF16),
            pltpu.SemaphoreType.DMA((CHUNKS, 2)),
            pltpu.SemaphoreType.DMA((CHUNKS, 2)),
            pltpu.SemaphoreType.DMA,
        ],
        compiler_params=pltpu.CompilerParams(vmem_limit_bytes=48 * MIB),
        name="y_there",
    )(idx, moment, factor)


def y_here(mine, ut):
    return pl.pallas_call(
        y_here_kernel,
        out_shape=jax.ShapeDtypeStruct((16, 128, 128), BF16),
        in_specs=[VMEM, VMEM],
        out_specs=VMEM,
        compiler_params=pltpu.CompilerParams(vmem_limit_bytes=16 * MIB),
        name="y_here",
    )(mine, ut)


def z_kernel(y_ref, u_ref, out_ref, w_ref, z_ref):
    w_ref[...] = jnp.zeros(w_ref.shape, BF16)
    for s in range(16):
        block = u_ref[64 * s : 64 * s + 64, :]
        w_ref[128 * s : 128 * s + 64, 0:128] = block
        w_ref[128 * s + 64 : 128 * s + 128, 128:256] = block
    lhs = jnp.concatenate([y_ref[s] for s in range(16)], axis=1)
    z = jnp.dot(lhs, w_ref[...], preferred_element_type=F32) * (1.0 / 32.0)
    z_ref[0] = z[:, 0:128]
    z_ref[1] = z[:, 128:256]
    for b in range(8):
        zb = [z_ref[i2, pl.ds(b, 16, stride=8), :] for i2 in range(2)]
        parts = []
        for q in range(4):
            cut = [
                zb[i2][8 * iph : 8 * iph + 8, 32 * q : 32 * q + 32]
                for i2 in range(2)
                for iph in range(2)
            ]
            parts.append(jnp.concatenate(cut, axis=1))
        out_ref[32 * b : 32 * b + 32, :] = jnp.concatenate(parts, axis=0).astype(BF16)


def v_kernel(z_ref, u_ref, out_ref, w_ref, v_ref):
    zt = z_ref[...]
    u = u_ref[...].astype(F32).reshape(32, 4, 8, 128)
    uw = jnp.concatenate([u[:, s].reshape(256, 128) for s in range(4)], axis=1).astype(BF16)
    full = lax.dot_general(zt, uw, (((0,), (0,)), ((), ())), preferred_element_type=F32)
    c = full[0:32, 0:128]
    for s in range(1, 4):
        c = c + full[32 * s : 32 * s + 32, 128 * s : 128 * s + 128]
    c = (c * (1.0 / 32.0)).astype(BF16)
    w_ref[...] = jnp.zeros(w_ref.shape, BF16)
    for s in range(4):
        w_ref[32 * s : 32 * s + 32, 128 * s : 128 * s + 128] = c
    v = jnp.dot(zt, w_ref[...], preferred_element_type=F32)
    for s in range(4):
        v_ref[s] = v[:, 128 * s : 128 * s + 128]
        for row in range(8):
            out_ref[8 * s + row] = v_ref[s, pl.ds(row, 32, stride=8), :]


def sum_kernel(in_ref, out_ref, mid_ref, low_ref, tail_ref):
    total = jnp.sum(in_ref[...], axis=0)
    high = total.astype(BF16).astype(F32)
    rest = total - high
    mid = rest.astype(BF16).astype(F32)
    mid_ref[...] = mid
    low_ref[...] = rest - mid
    tail_ref[...] = jnp.zeros(tail_ref.shape, F32)
    for d in range(16):
        tail_ref[d, 0:2, :] = mid_ref[2 * d : 2 * d + 2, :]
        tail_ref[d, 2:4, :] = low_ref[2 * d : 2 * d + 2, :]
    high = jnp.broadcast_to(high[None], (16, 32, 128))
    out_ref[...] = jnp.concatenate([high, tail_ref[...]], axis=1).astype(BF16)


def rows_kernel(idx_ref, in_ref, out_ref, v_ref):
    v = jnp.sum(in_ref[...].astype(F32), axis=0)
    v_ref[...] = v
    squares = jnp.sum(v[0:32] * v[0:32], axis=0, keepdims=True)
    own = v_ref[pl.ds(2 * (idx_ref[0] // 2), 2), :] + (v[32:34] + v[34:36])
    block = jnp.concatenate([own, squares, jnp.zeros((1, 128), F32)], axis=0)
    out_ref[...] = jnp.broadcast_to(block[None], out_ref.shape)


def final_kernel(in_ref, out_ref):
    total = jnp.sum(in_ref[pl.ds(2, 32, stride=4), :]) * (1.0 / (128.0 * 128.0))
    scale = lax.rsqrt(total / (1024 * 128) + 1e-06) * (1.0 / 128.0)
    out_ref[0:32, :] = in_ref[pl.ds(0, 32, stride=4), :] * scale
    out_ref[32:64, :] = in_ref[pl.ds(1, 32, stride=4), :] * scale


def call(kernel, out, specs, scratch, mib, name):
    return pl.pallas_call(
        kernel,
        out_shape=jax.ShapeDtypeStruct(*out),
        in_specs=specs,
        out_specs=VMEM,
        scratch_shapes=scratch,
        compiler_params=params(mib),
        name=name,
    )


def local(moment, factor):
    plane = ("gy", "gz")
    idx = (2 * lax.axis_index("gx") + lax.axis_index("gz")).astype(jnp.int32).reshape(1)
    there, ut, mine = y_there(idx, moment, factor)
    came = lax.ppermute(there, "gz", [(0, 1), (1, 0)])
    here = y_here(mine, ut)
    y = (here.astype(F32) + came.astype(F32)).astype(BF16)
    y = lax.all_to_all(y, "gy", 0, 0, tiled=True)
    z = call(
        z_kernel,
        ((256, 128), BF16),
        [VMEM, VMEM],
        [pltpu.VMEM((2048, 256), BF16), pltpu.VMEM((2, 128, 128), F32)],
        8,
        "z_block",
    )(y, factor)
    z = lax.all_to_all(z.reshape(32, 8, 128), ("gx", "gz"), 0, 0, tiled=True)
    v = call(
        v_kernel,
        ((32, 32, 128), F32),
        [VMEM, VMEM],
        [pltpu.VMEM((128, 512), BF16), pltpu.VMEM((4, 256, 128), F32)],
        8,
        "v_part",
    )(z.reshape(256, 128), factor)
    v = lax.all_to_all(v, plane, 0, 0, tiled=True)
    v = call(
        sum_kernel,
        ((16, 40, 128), BF16),
        [VMEM],
        [pltpu.VMEM((32, 128), F32), pltpu.VMEM((32, 128), F32), pltpu.VMEM((16, 8, 128), F32)],
        8,
        "v_sum_plane",
    )(v)
    v = lax.all_to_all(v, "gx", 0, 0, tiled=True)
    v = call(
        rows_kernel, ((32, 4, 128), F32), [SMEM, VMEM], [pltpu.VMEM((40, 128), F32)], 8, "v_rows"
    )(idx, v)
    v = lax.all_to_all(v, plane, 0, 0, tiled=True)
    return call(final_kernel, ((64, 128), F32), [VMEM], [], 8, "scaled")(v.reshape(128, 128))


def solution(mesh):
    in_specs = (P("gx", "gy", "gz"), P())
    out_specs = P("gx", None)
    return jax.shard_map(local, mesh=mesh, in_specs=in_specs, out_specs=out_specs, check_vma=False)
```

```python
import jax
import jax.numpy as jnp
from jax import lax
from jax.experimental import pallas as pl
from jax.experimental.pallas import tpu as pltpu
from jax.sharding import PartitionSpec as P

F32 = jnp.float32
BF16 = jnp.bfloat16
MIB = 1 << 20
VMEM = pl.BlockSpec(memory_space=pltpu.VMEM)
ANY = pl.BlockSpec(memory_space=pl.ANY)
SMEM = pl.BlockSpec(memory_space=pltpu.SMEM)


def params(mib):
    return pltpu.CompilerParams(vmem_limit_bytes=mib * MIB)


def y_store(ut, rows, first, out_ref):
    y = lax.dot_general(ut, rows, (((1,), (1,)), ((), ())), preferred_element_type=F32)
    parts = [y[:, n : n + 128].reshape(16, 8, 128) for n in range(0, y.shape[1], 128)]
    out_ref[:, 8 * first : 8 * (first + len(parts)), :] = jnp.concatenate(parts, axis=1).astype(BF16)


CHUNK = 8
CHUNKS = 16 // CHUNK
DOT = 2
HALF = (CHUNKS, 2, CHUNK, 64, 512)


def y_copies(half, m_ref, buf, sem):
    copies = []
    for t in range(CHUNKS):
        for h in range(2):
            block = m_ref.at[pl.ds(32 * half + 16 * h + CHUNK * t, CHUNK)]
            copies.append(pltpu.make_async_copy(block, buf.at[t, h], sem.at[t, h]))
            copies[-1].start()
    return copies


def y_chunk(t, ut, buf, out_ref):
    for p in range(0, CHUNK, DOT):
        rows = jnp.concatenate([buf[t, h, p + n] for n in range(DOT) for h in range(2)], axis=0)
        y_store(ut, rows, CHUNK * t + p, out_ref)


def stage_kernel(idx_ref, m_ref, theirs_ref, sem):
    for copy in y_copies(1 - lax.rem(idx_ref[0], 2), m_ref, theirs_ref, sem):
        copy.wait()


def y_there_kernel(idx_ref, theirs_ref, u_ref, out_ref, ut_ref):
    core = lax.rem(idx_ref[0], 2)
    ut_ref[...] = u_ref[pl.ds(pl.multiple_of(512 * core, 512), 512), :].T
    for t in range(CHUNKS):
        y_chunk(t, ut_ref[...], theirs_ref, out_ref)


def y_here_kernel(idx_ref, m_ref, ut_ref, out_ref, buf, sem):
    copies = y_copies(lax.rem(idx_ref[0], 2), m_ref, buf, sem)
    for t in range(CHUNKS):
        copies[2 * t].wait()
        copies[2 * t + 1].wait()
        y_chunk(t, ut_ref[...], buf, out_ref)


def y_there(idx, moment, factor):
    theirs = pl.pallas_call(
        stage_kernel,
        out_shape=jax.ShapeDtypeStruct(HALF, BF16),
        in_specs=[SMEM, ANY],
        out_specs=VMEM,
        scratch_shapes=[pltpu.SemaphoreType.DMA((CHUNKS, 2))],
        compiler_params=params(48),
        name="stage",
    )(idx, moment)
    return pl.pallas_call(
        y_there_kernel,
        out_shape=[jax.ShapeDtypeStruct((16, 128, 128), BF16), jax.ShapeDtypeStruct((128, 512), BF16)],
        in_specs=[SMEM, VMEM, VMEM],
        out_specs=[VMEM, VMEM],
        compiler_params=params(48),
        name="y_there",
    )(idx, theirs, factor)


def y_here(idx, moment, ut):
    return pl.pallas_call(
        y_here_kernel,
        out_shape=jax.ShapeDtypeStruct((16, 128, 128), BF16),
        in_specs=[SMEM, ANY, VMEM],
        out_specs=VMEM,
        scratch_shapes=[pltpu.VMEM(HALF, BF16), pltpu.SemaphoreType.DMA((CHUNKS, 2))],
        compiler_params=params(48),
        name="y_here",
    )(idx, moment, ut)


def z_kernel(y_ref, u_ref, out_ref, w_ref, z_ref):
    w_ref[...] = jnp.zeros(w_ref.shape, BF16)
    for s in range(16):
        block = u_ref[64 * s : 64 * s + 64, :]
        w_ref[128 * s : 128 * s + 64, 0:128] = block
        w_ref[128 * s + 64 : 128 * s + 128, 128:256] = block
    lhs = jnp.concatenate([y_ref[s] for s in range(16)], axis=1)
    z = jnp.dot(lhs, w_ref[...], preferred_element_type=F32) * (1.0 / 32.0)
    z_ref[0] = z[:, 0:128]
    z_ref[1] = z[:, 128:256]
    for b in range(8):
        zb = [z_ref[i2, pl.ds(b, 16, stride=8), :] for i2 in range(2)]
        parts = []
        for q in range(4):
            cut = [
                zb[i2][8 * iph : 8 * iph + 8, 32 * q : 32 * q + 32]
                for i2 in range(2)
                for iph in range(2)
            ]
            parts.append(jnp.concatenate(cut, axis=1))
        for q2 in range(2):
            block = jnp.concatenate(parts[2 * q2 : 2 * q2 + 2], axis=0).astype(BF16)
            out_ref[2 * b + q2] = block


def v_kernel(idx_ref, z_ref, u_ref, out_ref, w_ref, v_ref):
    core = lax.rem(idx_ref[0], 2)
    z = z_ref[...].astype(F32)
    zt = jnp.concatenate([z[:, 8 * q : 8 * q + 8].reshape(256, 128) for q in range(2)], axis=1).astype(BF16)
    u = u_ref[...].astype(F32).reshape(16, 2, 4, 8, 128)
    uw = [jnp.concatenate([u[:, h, s].reshape(128, 128) for h in range(2)], axis=0) for s in range(4)]
    uw = jnp.concatenate(uw, axis=1).astype(BF16)
    full = lax.dot_general(zt, uw, (((0,), (0,)), ((), ())), preferred_element_type=F32)
    w_ref[...] = jnp.zeros(w_ref.shape, BF16)
    for q in range(2):
        c = full[128 * q : 128 * q + 32, 0:128]
        for s in range(1, 4):
            c = c + full[128 * q + 32 * s : 128 * q + 32 * s + 32, 128 * s : 128 * s + 128]
        c = (c * (1.0 / 32.0)).astype(BF16)
        for s in range(2):
            w_ref[pl.ds(pl.multiple_of(128 * q + 64 * core + 32 * s, 32), 32), 128 * s : 128 * s + 128] = c
    v = jnp.dot(zt, w_ref[...], preferred_element_type=F32)
    for s in range(2):
        v_ref[s] = v[:, 128 * s : 128 * s + 128]
        for row in range(8):
            out_ref[8 * s + row] = v_ref[s, pl.ds(row, 32, stride=8), :]


def sum_kernel(in_ref, out_ref, mid_ref, low_ref, tail_ref):
    total = jnp.sum(in_ref[...], axis=0)
    high = total.astype(BF16).astype(F32)
    rest = total - high
    mid = rest.astype(BF16).astype(F32)
    mid_ref[...] = mid
    low_ref[...] = rest - mid
    tail_ref[...] = jnp.zeros(tail_ref.shape, F32)
    for d in range(16):
        for h in range(2):
            tail_ref[d, h : h + 1, :] = mid_ref[16 * h + d : 16 * h + d + 1, :]
            tail_ref[d, 2 + h : 3 + h, :] = low_ref[16 * h + d : 16 * h + d + 1, :]
    high = jnp.broadcast_to(high[None], (16, 32, 128))
    out_ref[...] = jnp.concatenate([high, tail_ref[...]], axis=1).astype(BF16)


def rows_kernel(idx_ref, in_ref, out_ref, v_ref):
    v = jnp.sum(in_ref[...].astype(F32), axis=0)
    v_ref[...] = v
    squares = jnp.sum(v[0:32] * v[0:32], axis=0, keepdims=True)
    block = idx_ref[0] // 2
    own = jnp.concatenate([v_ref[pl.ds(block, 1), :], v_ref[pl.ds(16 + block, 1), :]], axis=0)
    own = own + (v[32:34] + v[34:36])
    message = jnp.concatenate([own, squares, jnp.zeros((1, 128), F32)], axis=0)
    out_ref[...] = jnp.broadcast_to(message[None], out_ref.shape)


def final_kernel(in_ref, out_ref):
    total = jnp.sum(in_ref[pl.ds(2, 32, stride=4), :]) * (1.0 / (128.0 * 128.0))
    scale = lax.rsqrt(total / (1024 * 128) + 1e-06) * (1.0 / 128.0)
    for half in range(2):
        for core in range(2):
            for s in range(2):
                rows = in_ref[pl.ds(64 * s + 4 * core + half, 8, stride=8), :]
                first = 32 * half + 16 * core + 8 * s
                out_ref[first : first + 8, :] = rows * scale


def call(kernel, out, specs, scratch, mib, name):
    return pl.pallas_call(
        kernel,
        out_shape=jax.ShapeDtypeStruct(*out),
        in_specs=specs,
        out_specs=VMEM,
        scratch_shapes=scratch,
        compiler_params=params(mib),
        name=name,
    )


def local(moment, factor):
    plane = ("gy", "gz")
    idx = (2 * lax.axis_index("gx") + lax.axis_index("gz")).astype(jnp.int32).reshape(1)
    there, ut = y_there(idx, moment, factor)
    came = lax.ppermute(there, "gz", [(0, 1), (1, 0)])
    here = y_here(idx, moment, ut)
    y = (here.astype(F32) + came.astype(F32)).astype(BF16)
    y = lax.all_to_all(y, "gy", 0, 0, tiled=True)
    z = call(
        z_kernel,
        ((16, 16, 128), BF16),
        [VMEM, VMEM],
        [pltpu.VMEM((2048, 256), BF16), pltpu.VMEM((2, 128, 128), F32)],
        8,
        "z_block",
    )(y, factor)
    z = lax.all_to_all(z, "gx", 0, 0, tiled=True)
    z = lax.all_gather(z, "gz", axis=0, tiled=True)
    v = call(
        v_kernel,
        ((16, 32, 128), F32),
        [SMEM, VMEM, VMEM],
        [pltpu.VMEM((256, 256), BF16), pltpu.VMEM((2, 256, 128), F32)],
        8,
        "v_part",
    )(idx, z, factor)
    v = lax.all_to_all(v, "gy", 0, 0, tiled=True)
    v = call(
        sum_kernel,
        ((16, 40, 128), BF16),
        [VMEM],
        [pltpu.VMEM((32, 128), F32), pltpu.VMEM((32, 128), F32), pltpu.VMEM((16, 8, 128), F32)],
        8,
        "v_sum_plane",
    )(v)
    v = lax.all_to_all(v, "gx", 0, 0, tiled=True)
    v = call(
        rows_kernel, ((32, 4, 128), F32), [SMEM, VMEM], [pltpu.VMEM((40, 128), F32)], 8, "v_rows"
    )(idx, v)
    v = lax.all_to_all(v, plane, 0, 0, tiled=True)
    return call(final_kernel, ((64, 128), F32), [VMEM], [], 8, "scaled")(v.reshape(128, 128))


def solution(mesh):
    in_specs = (P("gx", "gy", "gz"), P())
    out_specs = P("gx", None)
    return jax.shard_map(local, mesh=mesh, in_specs=in_specs, out_specs=out_specs, check_vma=False)
```

```python
import jax
import jax.numpy as jnp
from jax import lax
from jax.experimental import pallas as pl
from jax.experimental.pallas import tpu as pltpu
from jax.sharding import PartitionSpec as P

F32 = jnp.float32
BF16 = jnp.bfloat16
MIB = 1 << 20
VMEM = pl.BlockSpec(memory_space=pltpu.VMEM)
ANY = pl.BlockSpec(memory_space=pl.ANY)
SMEM = pl.BlockSpec(memory_space=pltpu.SMEM)


def params(mib):
    return pltpu.CompilerParams(vmem_limit_bytes=mib * MIB)


def y_store(ut, rows, first, out_ref):
    y = lax.dot_general(ut, rows, (((1,), (1,)), ((), ())), preferred_element_type=F32)
    parts = [y[:, n : n + 128].reshape(16, 8, 128) for n in range(0, y.shape[1], 128)]
    out_ref[:, 8 * first : 8 * (first + len(parts)), :] = jnp.concatenate(parts, axis=1).astype(BF16)


CHUNK = 8
CHUNKS = 16 // CHUNK
DOT = 2
HALF = (CHUNKS, 2, CHUNK, 64, 512)


def y_copies(half, m_ref, buf, sem):
    copies = []
    for t in range(CHUNKS):
        for h in range(2):
            block = m_ref.at[pl.ds(32 * half + 16 * h + CHUNK * t, CHUNK)]
            copies.append(pltpu.make_async_copy(block, buf.at[t, h], sem.at[t, h]))
            copies[-1].start()
    return copies


def y_chunk(t, ut, buf, out_ref):
    for p in range(0, CHUNK, DOT):
        rows = jnp.concatenate([buf[t, h, p + n] for n in range(DOT) for h in range(2)], axis=0)
        y_store(ut, rows, CHUNK * t + p, out_ref)


def stage_kernel(idx_ref, m_ref, theirs_ref, sem):
    for copy in y_copies(1 - lax.rem(idx_ref[0], 2), m_ref, theirs_ref, sem):
        copy.wait()


def y_there_kernel(idx_ref, theirs_ref, u_ref, out_ref, ut_ref):
    core = lax.rem(idx_ref[0], 2)
    ut_ref[...] = u_ref[pl.ds(pl.multiple_of(512 * core, 512), 512), :].T
    for t in range(CHUNKS):
        y_chunk(t, ut_ref[...], theirs_ref, out_ref)


def y_here_kernel(idx_ref, m_ref, ut_ref, out_ref, buf, sem):
    copies = y_copies(lax.rem(idx_ref[0], 2), m_ref, buf, sem)
    for t in range(CHUNKS):
        copies[2 * t].wait()
        copies[2 * t + 1].wait()
        y_chunk(t, ut_ref[...], buf, out_ref)


def y_there(idx, moment, factor):
    theirs = pl.pallas_call(
        stage_kernel,
        out_shape=jax.ShapeDtypeStruct(HALF, BF16),
        in_specs=[SMEM, ANY],
        out_specs=VMEM,
        scratch_shapes=[pltpu.SemaphoreType.DMA((CHUNKS, 2))],
        compiler_params=params(48),
        name="stage",
    )(idx, moment)
    return pl.pallas_call(
        y_there_kernel,
        out_shape=[jax.ShapeDtypeStruct((16, 128, 128), BF16), jax.ShapeDtypeStruct((128, 512), BF16)],
        in_specs=[SMEM, VMEM, VMEM],
        out_specs=[VMEM, VMEM],
        compiler_params=params(48),
        name="y_there",
    )(idx, theirs, factor)


def y_here(idx, moment, ut):
    return pl.pallas_call(
        y_here_kernel,
        out_shape=jax.ShapeDtypeStruct((16, 128, 128), BF16),
        in_specs=[SMEM, ANY, VMEM],
        out_specs=VMEM,
        scratch_shapes=[pltpu.VMEM(HALF, BF16), pltpu.SemaphoreType.DMA((CHUNKS, 2))],
        compiler_params=params(48),
        name="y_here",
    )(idx, moment, ut)


def z_kernel(y_ref, u_ref, out_ref, w_ref, z_ref):
    w_ref[...] = jnp.zeros(w_ref.shape, BF16)
    for s in range(16):
        block = u_ref[64 * s : 64 * s + 64, :]
        w_ref[128 * s : 128 * s + 64, 0:128] = block
        w_ref[128 * s + 64 : 128 * s + 128, 128:256] = block
    lhs = jnp.concatenate([y_ref[s] for s in range(16)], axis=1)
    z = jnp.dot(lhs, w_ref[...], preferred_element_type=F32) * (1.0 / 32.0)
    z_ref[0] = z[:, 0:128]
    z_ref[1] = z[:, 128:256]
    for b in range(8):
        zb = [z_ref[i2, pl.ds(b, 16, stride=8), :] for i2 in range(2)]
        parts = []
        for q in range(4):
            cut = [
                zb[i2][8 * iph : 8 * iph + 8, 32 * q : 32 * q + 32]
                for i2 in range(2)
                for iph in range(2)
            ]
            parts.append(jnp.concatenate(cut, axis=1))
        for q2 in range(2):
            block = jnp.concatenate(parts[2 * q2 : 2 * q2 + 2], axis=0).astype(BF16)
            out_ref[2 * b + q2] = block


def v_kernel(idx_ref, z_ref, u_ref, out_ref, w_ref, v_ref):
    core = lax.rem(idx_ref[0], 2)
    z = z_ref[...].astype(F32)
    zt = jnp.concatenate([z[:, 8 * q : 8 * q + 8].reshape(256, 128) for q in range(2)], axis=1).astype(BF16)
    u = u_ref[...].astype(F32).reshape(16, 2, 4, 8, 128)
    uw = [jnp.concatenate([u[:, h, s].reshape(128, 128) for h in range(2)], axis=0) for s in range(4)]
    uw = jnp.concatenate(uw, axis=1).astype(BF16)
    full = lax.dot_general(zt, uw, (((0,), (0,)), ((), ())), preferred_element_type=F32)
    w_ref[...] = jnp.zeros(w_ref.shape, BF16)
    for q in range(2):
        c = full[128 * q : 128 * q + 32, 0:128]
        for s in range(1, 4):
            c = c + full[128 * q + 32 * s : 128 * q + 32 * s + 32, 128 * s : 128 * s + 128]
        c = (c * (1.0 / 32.0)).astype(BF16)
        for s in range(2):
            w_ref[pl.ds(pl.multiple_of(128 * q + 64 * core + 32 * s, 32), 32), 128 * s : 128 * s + 128] = c
    v = jnp.dot(zt, w_ref[...], preferred_element_type=F32)
    for s in range(2):
        v_ref[s] = v[:, 128 * s : 128 * s + 128]
        for row in range(8):
            out_ref[8 * s + row] = v_ref[s, pl.ds(row, 32, stride=8), :]


def sum_kernel(in_ref, out_ref, mid_ref, low_ref, tail_ref):
    total = jnp.sum(in_ref[...], axis=0) * (1.0 / 128.0)
    high = total.astype(BF16).astype(F32)
    rest = total - high
    mid = rest.astype(BF16).astype(F32)
    mid_ref[...] = mid
    low_ref[...] = rest - mid
    for k in range(4):
        group = high[8 * k : 8 * k + 8]
        size = jnp.sum(group * group, axis=0, keepdims=True)
        error = jnp.sum(group * rest[8 * k : 8 * k + 8], axis=0, keepdims=True)
        ratio = jnp.where(size > 0.0, error / jnp.where(size > 0.0, size, 1.0), 0.0)
        ratio = jnp.clip(ratio, -(2.0**-8), 2.0**-8)
        for d in range(16):
            tail_ref[d, k : k + 1, :] = ratio
    for d in range(16):
        for h in range(2):
            tail_ref[d, 4 + h : 5 + h, :] = mid_ref[16 * h + d : 16 * h + d + 1, :]
            tail_ref[d, 6 + h : 7 + h, :] = low_ref[16 * h + d : 16 * h + d + 1, :]
    high = jnp.broadcast_to(high[None], (16, 32, 128))
    out_ref[...] = jnp.concatenate([high, tail_ref[...]], axis=1).astype(BF16)


def rows_kernel(idx_ref, in_ref, out_ref, v_ref):
    parts = in_ref[...].astype(F32)
    v = jnp.sum(parts, axis=0)
    v_ref[...] = v
    squares = jnp.zeros((8, 128), F32)
    for k in range(4):
        group = parts[:, 8 * k : 8 * k + 8]
        rows = v[8 * k : 8 * k + 8] + jnp.sum(group * parts[:, 32 + k : 33 + k], axis=0)
        squares = squares + rows * rows
    squares = jnp.sum(squares, axis=0, keepdims=True)
    block = idx_ref[0] // 2
    own = jnp.concatenate([v_ref[pl.ds(block, 1), :], v_ref[pl.ds(16 + block, 1), :]], axis=0)
    own = own + (v[36:38] + v[38:40])
    message = jnp.concatenate([own, squares, jnp.zeros((1, 128), F32)], axis=0)
    out_ref[...] = jnp.broadcast_to(message[None], out_ref.shape)


def final_kernel(in_ref, out_ref):
    total = jnp.sum(in_ref[pl.ds(2, 32, stride=4), :])
    scale = lax.rsqrt(total / (1024 * 128) + 1e-06)
    for half in range(2):
        for core in range(2):
            for s in range(2):
                rows = in_ref[pl.ds(64 * s + 4 * core + half, 8, stride=8), :]
                first = 32 * half + 16 * core + 8 * s
                out_ref[first : first + 8, :] = rows * scale


def call(kernel, out, specs, scratch, mib, name):
    return pl.pallas_call(
        kernel,
        out_shape=jax.ShapeDtypeStruct(*out),
        in_specs=specs,
        out_specs=VMEM,
        scratch_shapes=scratch,
        compiler_params=params(mib),
        name=name,
    )


def local(moment, factor):
    plane = ("gy", "gz")
    idx = (2 * lax.axis_index("gx") + lax.axis_index("gz")).astype(jnp.int32).reshape(1)
    there, ut = y_there(idx, moment, factor)
    came = lax.ppermute(there, "gz", [(0, 1), (1, 0)])
    here = y_here(idx, moment, ut)
    y = (here.astype(F32) + came.astype(F32)).astype(BF16)
    y = lax.all_to_all(y, "gy", 0, 0, tiled=True)
    z = call(
        z_kernel,
        ((16, 16, 128), BF16),
        [VMEM, VMEM],
        [pltpu.VMEM((2048, 256), BF16), pltpu.VMEM((2, 128, 128), F32)],
        8,
        "z_block",
    )(y, factor)
    z = lax.all_to_all(z, "gx", 0, 0, tiled=True)
    z = lax.all_gather(z, "gz", axis=0, tiled=True)
    v = call(
        v_kernel,
        ((16, 32, 128), F32),
        [SMEM, VMEM, VMEM],
        [pltpu.VMEM((256, 256), BF16), pltpu.VMEM((2, 256, 128), F32)],
        8,
        "v_part",
    )(idx, z, factor)
    v = lax.all_to_all(v, "gy", 0, 0, tiled=True)
    v = call(
        sum_kernel,
        ((16, 40, 128), BF16),
        [VMEM],
        [pltpu.VMEM((32, 128), F32), pltpu.VMEM((32, 128), F32), pltpu.VMEM((16, 8, 128), F32)],
        8,
        "v_sum_plane",
    )(v)
    v = lax.all_to_all(v, "gx", 0, 0, tiled=True)
    v = call(
        rows_kernel, ((32, 4, 128), F32), [SMEM, VMEM], [pltpu.VMEM((40, 128), F32)], 8, "v_rows"
    )(idx, v)
    v = lax.all_to_all(v, plane, 0, 0, tiled=True)
    return call(final_kernel, ((64, 128), F32), [VMEM], [], 8, "scaled")(v.reshape(128, 128))


def solution(mesh):
    in_specs = (P("gx", "gy", "gz"), P())
    out_specs = P("gx", None)
    return jax.shard_map(local, mesh=mesh, in_specs=in_specs, out_specs=out_specs, check_vma=False)
```

```python
import jax
import jax.numpy as jnp
from jax import lax
from jax.experimental import pallas as pl
from jax.experimental.pallas import tpu as pltpu
from jax.sharding import PartitionSpec as P

F32 = jnp.float32
BF16 = jnp.bfloat16
MIB = 1 << 20
VMEM = pl.BlockSpec(memory_space=pltpu.VMEM)
ANY = pl.BlockSpec(memory_space=pl.ANY)
SMEM = pl.BlockSpec(memory_space=pltpu.SMEM)


def params(mib):
    return pltpu.CompilerParams(vmem_limit_bytes=mib * MIB)


def y_store(ut, rows, first, out_ref):
    y = lax.dot_general(ut, rows, (((1,), (1,)), ((), ())), preferred_element_type=F32)
    parts = [y[:, n : n + 128].reshape(16, 8, 128) for n in range(0, y.shape[1], 128)]
    out_ref[:, 8 * first : 8 * (first + len(parts)), :] = jnp.concatenate(parts, axis=1).astype(BF16)


CHUNK = 8
CHUNKS = 16 // CHUNK
DOT = 2
HALF = (CHUNKS, 2, CHUNK, 64, 512)


def y_copies(half, m_ref, buf, sem):
    copies = []
    for t in range(CHUNKS):
        for h in range(2):
            block = m_ref.at[pl.ds(32 * half + 16 * h + CHUNK * t, CHUNK)]
            copies.append(pltpu.make_async_copy(block, buf.at[t, h], sem.at[t, h]))
            copies[-1].start()
    return copies


def y_chunk(t, ut, buf, out_ref):
    for p in range(0, CHUNK, DOT):
        rows = jnp.concatenate([buf[t, h, p + n] for n in range(DOT) for h in range(2)], axis=0)
        y_store(ut, rows, CHUNK * t + p, out_ref)


def stage_kernel(idx_ref, m_ref, theirs_ref, sem):
    for copy in y_copies(1 - lax.rem(idx_ref[0], 2), m_ref, theirs_ref, sem):
        copy.wait()


def y_there_kernel(idx_ref, theirs_ref, u_ref, out_ref, ut_ref):
    core = lax.rem(idx_ref[0], 2)
    ut_ref[...] = u_ref[pl.ds(pl.multiple_of(512 * core, 512), 512), :].T
    for t in range(CHUNKS):
        y_chunk(t, ut_ref[...], theirs_ref, out_ref)


def y_here_kernel(idx_ref, m_ref, ut_ref, out_ref, buf, sem):
    copies = y_copies(lax.rem(idx_ref[0], 2), m_ref, buf, sem)
    for t in range(CHUNKS):
        copies[2 * t].wait()
        copies[2 * t + 1].wait()
        y_chunk(t, ut_ref[...], buf, out_ref)


def y_there(idx, moment, factor):
    theirs = pl.pallas_call(
        stage_kernel,
        out_shape=jax.ShapeDtypeStruct(HALF, BF16),
        in_specs=[SMEM, ANY],
        out_specs=VMEM,
        scratch_shapes=[pltpu.SemaphoreType.DMA((CHUNKS, 2))],
        compiler_params=params(48),
        name="stage",
    )(idx, moment)
    return pl.pallas_call(
        y_there_kernel,
        out_shape=[jax.ShapeDtypeStruct((16, 128, 128), BF16), jax.ShapeDtypeStruct((128, 512), BF16)],
        in_specs=[SMEM, VMEM, VMEM],
        out_specs=[VMEM, VMEM],
        compiler_params=params(48),
        name="y_there",
    )(idx, theirs, factor)


def y_here(idx, moment, ut):
    return pl.pallas_call(
        y_here_kernel,
        out_shape=jax.ShapeDtypeStruct((16, 128, 128), BF16),
        in_specs=[SMEM, ANY, VMEM],
        out_specs=VMEM,
        scratch_shapes=[pltpu.VMEM(HALF, BF16), pltpu.SemaphoreType.DMA((CHUNKS, 2))],
        compiler_params=params(48),
        name="y_here",
    )(idx, moment, ut)


def z_kernel(y_ref, u_ref, out_ref, z_ref):
    lhs = []
    for i2 in range(2):
        cut = [y_ref[s][:, 64 * i2 : 64 * i2 + 64] for s in range(16)]
        lhs.append(jnp.concatenate(cut, axis=1))
    z = jnp.dot(jnp.concatenate(lhs, axis=0), u_ref[...], preferred_element_type=F32) * (1.0 / 32.0)
    z_ref[0] = z[0:128]
    z_ref[1] = z[128:256]
    for b in range(8):
        low, high = [z_ref[i2, pl.ds(b, 16, stride=8), :] for i2 in range(2)]
        out_ref[2 * b] = jnp.concatenate([low[:, 0:64], high[:, 0:64]], axis=1).astype(BF16)
        out_ref[2 * b + 1] = jnp.concatenate([low[:, 64:128], high[:, 64:128]], axis=1).astype(BF16)


def v_kernel(idx_ref, z_ref, u_ref, out_ref, w_ref, v_ref):
    core = lax.rem(idx_ref[0], 2)
    u = u_ref[...].reshape(16, 4, 16, 128)
    uw = [jnp.concatenate([u[:, 2 * h + i2].reshape(256, 128) for h in range(2)], axis=0) for i2 in range(2)]
    uw = jnp.concatenate(uw, axis=1)
    zt = z_ref[...]
    full = lax.dot_general(zt, uw, (((0,), (0,)), ((), ())), preferred_element_type=F32)
    c = (full[0:64, 0:128] + full[64:128, 128:256]) * (1.0 / 32.0)
    w_ref[...] = jnp.zeros(w_ref.shape, BF16)
    w_ref[pl.ds(pl.multiple_of(64 * core, 64), 64), :] = c.astype(BF16)
    v_ref[...] = jnp.dot(zt, w_ref[...], preferred_element_type=F32)
    for ip in range(16):
        out_ref[ip] = v_ref[pl.ds(ip, 32, stride=16), :]


def sum_kernel(in_ref, out_ref, mid_ref, low_ref, tail_ref):
    total = jnp.sum(in_ref[...], axis=0) * (1.0 / 128.0)
    high = total.astype(BF16).astype(F32)
    rest = total - high
    mid = rest.astype(BF16).astype(F32)
    mid_ref[...] = mid
    low_ref[...] = rest - mid
    for k in range(4):
        group = high[8 * k : 8 * k + 8]
        size = jnp.sum(group * group, axis=0, keepdims=True)
        error = jnp.sum(group * rest[8 * k : 8 * k + 8], axis=0, keepdims=True)
        ratio = jnp.where(size > 0.0, error / jnp.where(size > 0.0, size, 1.0), 0.0)
        ratio = jnp.clip(ratio, -(2.0**-8), 2.0**-8)
        for d in range(16):
            tail_ref[d, k : k + 1, :] = ratio
    for d in range(16):
        for h in range(2):
            tail_ref[d, 4 + h : 5 + h, :] = mid_ref[16 * h + d : 16 * h + d + 1, :]
            tail_ref[d, 6 + h : 7 + h, :] = low_ref[16 * h + d : 16 * h + d + 1, :]
    high = jnp.broadcast_to(high[None], (16, 32, 128))
    out_ref[...] = jnp.concatenate([high, tail_ref[...]], axis=1).astype(BF16)


def rows_kernel(idx_ref, in_ref, out_ref, v_ref):
    parts = in_ref[...].astype(F32)
    v = jnp.sum(parts, axis=0)
    v_ref[...] = v
    squares = jnp.zeros((8, 128), F32)
    for k in range(4):
        group = parts[:, 8 * k : 8 * k + 8]
        rows = v[8 * k : 8 * k + 8] + jnp.sum(group * parts[:, 32 + k : 33 + k], axis=0)
        squares = squares + rows * rows
    squares = jnp.sum(squares, axis=0, keepdims=True)
    block = idx_ref[0] // 2
    own = jnp.concatenate([v_ref[pl.ds(block, 1), :], v_ref[pl.ds(16 + block, 1), :]], axis=0)
    own = own + (v[36:38] + v[38:40])
    message = jnp.concatenate([own, squares, jnp.zeros((1, 128), F32)], axis=0)
    out_ref[...] = jnp.broadcast_to(message[None], out_ref.shape)


def final_kernel(in_ref, out_ref):
    total = jnp.sum(in_ref[pl.ds(2, 32, stride=4), :])
    scale = lax.rsqrt(total / (1024 * 128) + 1e-06)
    for half in range(2):
        for core in range(2):
            first = 32 * half + 16 * core
            out_ref[first : first + 16, :] = in_ref[pl.ds(4 * core + half, 16, stride=8), :] * scale


def call(kernel, out, specs, scratch, mib, name):
    return pl.pallas_call(
        kernel,
        out_shape=jax.ShapeDtypeStruct(*out),
        in_specs=specs,
        out_specs=VMEM,
        scratch_shapes=scratch,
        compiler_params=params(mib),
        name=name,
    )


def local(moment, factor):
    plane = ("gy", "gz")
    idx = (2 * lax.axis_index("gx") + lax.axis_index("gz")).astype(jnp.int32).reshape(1)
    there, ut = y_there(idx, moment, factor)
    came = lax.ppermute(there, "gz", [(0, 1), (1, 0)])
    here = y_here(idx, moment, ut)
    y = (here.astype(F32) + came.astype(F32)).astype(BF16)
    y = lax.all_to_all(y, "gy", 0, 0, tiled=True)
    z = call(
        z_kernel,
        ((16, 16, 128), BF16),
        [VMEM, VMEM],
        [pltpu.VMEM((2, 128, 128), F32)],
        8,
        "z_block",
    )(y, factor)
    z = lax.all_to_all(z, "gx", 0, 0, tiled=True)
    z = lax.all_gather(z, "gz", axis=0, tiled=True)
    v = call(
        v_kernel,
        ((16, 32, 128), F32),
        [SMEM, VMEM, VMEM],
        [pltpu.VMEM((128, 128), BF16), pltpu.VMEM((512, 128), F32)],
        8,
        "v_part",
    )(idx, z.reshape(512, 128), factor)
    v = lax.all_to_all(v, "gy", 0, 0, tiled=True)
    v = call(
        sum_kernel,
        ((16, 40, 128), BF16),
        [VMEM],
        [pltpu.VMEM((32, 128), F32), pltpu.VMEM((32, 128), F32), pltpu.VMEM((16, 8, 128), F32)],
        8,
        "v_sum_plane",
    )(v)
    v = lax.all_to_all(v, "gx", 0, 0, tiled=True)
    v = call(
        rows_kernel, ((32, 4, 128), F32), [SMEM, VMEM], [pltpu.VMEM((40, 128), F32)], 8, "v_rows"
    )(idx, v)
    v = lax.all_to_all(v, plane, 0, 0, tiled=True)
    return call(final_kernel, ((64, 128), F32), [VMEM], [], 8, "scaled")(v.reshape(128, 128))


def solution(mesh):
    in_specs = (P("gx", "gy", "gz"), P())
    out_specs = P("gx", None)
    return jax.shard_map(local, mesh=mesh, in_specs=in_specs, out_specs=out_specs, check_vma=False)
```

```python
import functools

import jax
import jax.numpy as jnp
from jax import lax
from jax.experimental import pallas as pl
from jax.experimental.pallas import tpu as pltpu
from jax.sharding import PartitionSpec as P

F32 = jnp.float32
BF16 = jnp.bfloat16
MIB = 1 << 20
VMEM = pl.BlockSpec(memory_space=pltpu.VMEM)
ANY = pl.BlockSpec(memory_space=pl.ANY)
SMEM = pl.BlockSpec(memory_space=pltpu.SMEM)


def params(mib):
    return pltpu.CompilerParams(vmem_limit_bytes=mib * MIB)


def y_store(ut, rows, first, out_ref):
    y = lax.dot_general(ut, rows, (((1,), (1,)), ((), ())), preferred_element_type=F32)
    parts = [y[:, n : n + 128].reshape(16, 8, 128) for n in range(0, y.shape[1], 128)]
    out_ref[:, 8 * first : 8 * (first + len(parts)), :] = jnp.concatenate(parts, axis=1).astype(BF16)


CHUNK = 8
CHUNKS = 16 // CHUNK
DOT = 2
HALF = (CHUNKS, 2, CHUNK, 64, 512)


def y_copies(half, m_ref, buf, sem):
    copies = []
    for t in range(CHUNKS):
        for h in range(2):
            block = m_ref.at[pl.ds(32 * half + 16 * h + CHUNK * t, CHUNK)]
            copies.append(pltpu.make_async_copy(block, buf.at[t, h], sem.at[t, h]))
            copies[-1].start()
    return copies


def y_chunk(t, ut, buf, out_ref):
    for p in range(0, CHUNK, DOT):
        rows = jnp.concatenate([buf[t, h, p + n] for n in range(DOT) for h in range(2)], axis=0)
        y_store(ut, rows, CHUNK * t + p, out_ref)


def stage_kernel(first_core_ref, m_ref, theirs_ref, sem):
    for copy in y_copies(first_core_ref[0], m_ref, theirs_ref, sem):
        copy.wait()


def y_there_kernel(idx_ref, theirs_ref, u_ref, out_ref, ut_ref):
    core = lax.rem(idx_ref[0], 2)
    ut_ref[...] = u_ref[pl.ds(pl.multiple_of(512 * core, 512), 512), :].T
    for t in range(CHUNKS):
        y_chunk(t, ut_ref[...], theirs_ref, out_ref)


def y_here_kernel(idx_ref, m_ref, ut_ref, out_ref, buf, sem):
    copies = y_copies(lax.rem(idx_ref[0], 2), m_ref, buf, sem)
    for t in range(CHUNKS):
        copies[2 * t].wait()
        copies[2 * t + 1].wait()
        y_chunk(t, ut_ref[...], buf, out_ref)


def y_there(idx, first_core, moment, factor):
    theirs = pl.pallas_call(
        stage_kernel,
        out_shape=jax.ShapeDtypeStruct(HALF, BF16),
        in_specs=[SMEM, ANY],
        out_specs=VMEM,
        scratch_shapes=[pltpu.SemaphoreType.DMA((CHUNKS, 2))],
        compiler_params=params(48),
        name="stage",
    )(first_core, moment)
    return pl.pallas_call(
        y_there_kernel,
        out_shape=[jax.ShapeDtypeStruct((16, 128, 128), BF16), jax.ShapeDtypeStruct((128, 512), BF16)],
        in_specs=[SMEM, VMEM, VMEM],
        out_specs=[VMEM, VMEM],
        compiler_params=params(48),
        name="y_there",
    )(idx, theirs, factor)


def y_here(idx, moment, ut):
    return pl.pallas_call(
        y_here_kernel,
        out_shape=jax.ShapeDtypeStruct((16, 128, 128), BF16),
        in_specs=[SMEM, ANY, VMEM],
        out_specs=VMEM,
        scratch_shapes=[pltpu.VMEM(HALF, BF16), pltpu.SemaphoreType.DMA((CHUNKS, 2))],
        compiler_params=params(48),
        name="y_here",
    )(idx, moment, ut)


def z_kernel(y_ref, u_ref, out_ref, z_ref):
    lhs = []
    for i2 in range(2):
        cut = [y_ref[s][:, 64 * i2 : 64 * i2 + 64] for s in range(16)]
        lhs.append(jnp.concatenate(cut, axis=1))
    z = jnp.dot(jnp.concatenate(lhs, axis=0), u_ref[...], preferred_element_type=F32) * (1.0 / 32.0)
    z_ref[0] = z[0:128]
    z_ref[1] = z[128:256]
    for b in range(8):
        low, high = [z_ref[i2, pl.ds(b, 16, stride=8), :] for i2 in range(2)]
        out_ref[2 * b] = jnp.concatenate([low[:, 0:64], high[:, 0:64]], axis=1).astype(BF16)
        out_ref[2 * b + 1] = jnp.concatenate([low[:, 64:128], high[:, 64:128]], axis=1).astype(BF16)


SHARES = (((0, 0),), ((0, 1), (1, 0), (1, 1)))


def v_kernel(share, z_ref, u_ref, out_ref, w_ref, v_ref):
    u = u_ref[...].reshape(16, 4, 16, 128)
    uw = [jnp.concatenate([u[:, 2 * h + i2].reshape(256, 128) for h in range(2)], axis=0) for i2 in range(2)]
    uw = jnp.concatenate(uw, axis=1)
    full = lax.dot_general(z_ref[...], uw, (((0,), (0,)), ((), ())), preferred_element_type=F32)
    c = ((full[0:64, 0:128] + full[64:128, 128:256]) * (1.0 / 32.0)).astype(BF16)
    w_ref[...] = jnp.zeros(w_ref.shape, BF16)
    w_ref[0, 0:64] = c
    w_ref[1, 64:128] = c
    for n, (half, i2) in enumerate(share):
        rows = z_ref[256 * half : 256 * half + 256, :]
        v_ref[n] = jnp.dot(rows, w_ref[i2], preferred_element_type=F32)
        for ip in range(16):
            out_ref[ip, 16 * n : 16 * n + 16, :] = v_ref[n, pl.ds(ip, 16, stride=16), :]


def sum_kernel(in_ref, out_ref, mid_ref, tail_ref):
    total = jnp.sum(in_ref[...], axis=0) * (1.0 / 128.0)
    count = total.shape[0] // 16
    high = total.astype(BF16).astype(F32)
    rest = total - high
    mid_ref[...] = rest
    tail_ref[...] = jnp.zeros(tail_ref.shape, F32)
    for n in range(count):
        group = high[16 * n : 16 * n + 16]
        size = jnp.sum(group * group, axis=0, keepdims=True)
        error = jnp.sum(group * rest[16 * n : 16 * n + 16], axis=0, keepdims=True)
        ratio = jnp.where(size > 0.0, error / jnp.where(size > 0.0, size, 1.0), 0.0)
        ratio = jnp.clip(ratio, -(2.0**-8), 2.0**-8)
        for d in range(16):
            tail_ref[d, n : n + 1, :] = ratio
            tail_ref[d, count + n : count + n + 1, :] = mid_ref[16 * n + d : 16 * n + d + 1, :]
    high = jnp.broadcast_to(high[None], (16,) + high.shape)
    out_ref[...] = jnp.concatenate([high, tail_ref[...]], axis=1).astype(BF16)


def rows_kernel(count, idx_ref, in_ref, out_ref, v_ref):
    parts = in_ref[...].astype(F32)
    v = jnp.sum(parts, axis=0)
    v_ref[...] = v
    first = 16 * count
    squares = jnp.zeros((16, 128), F32)
    for n in range(count):
        group = parts[:, 16 * n : 16 * n + 16]
        rows = v[16 * n : 16 * n + 16] + jnp.sum(group * parts[:, first + n : first + n + 1], axis=0)
        squares = squares + rows * rows
    squares = jnp.sum(squares, axis=0, keepdims=True)
    block = idx_ref[0] // 2
    own = jnp.concatenate([v_ref[pl.ds(16 * n + block, 1), :] for n in range(count)], axis=0)
    own = own + v[first + count : first + 2 * count]
    own = [own] if count == 3 else [own, jnp.zeros((3 - count, 128), F32)]
    message = jnp.concatenate(own + [squares], axis=0)
    out_ref[...] = jnp.broadcast_to(message[None], out_ref.shape)


def final_kernel(in_ref, out_ref):
    total = jnp.sum(in_ref[pl.ds(3, 32, stride=4), :])
    scale = lax.rsqrt(total / (1024 * 128) + 1e-06)
    for core, share in enumerate(SHARES):
        for n, (half, i2) in enumerate(share):
            first = 32 * half + 16 * i2
            out_ref[first : first + 16, :] = in_ref[pl.ds(4 * core + n, 16, stride=8), :] * scale


def call(kernel, out, specs, scratch, mib, name):
    return pl.pallas_call(
        kernel,
        out_shape=jax.ShapeDtypeStruct(*out),
        in_specs=specs,
        out_specs=VMEM,
        scratch_shapes=scratch,
        compiler_params=params(mib),
        name=name,
    )


def v_share(share, idx, z, factor):
    count = len(share)
    tail = -(-2 * count // 8) * 8
    v = call(
        functools.partial(v_kernel, share),
        ((16, 16 * count, 128), F32),
        [VMEM, VMEM],
        [pltpu.VMEM((2, 128, 128), BF16), pltpu.VMEM((count, 256, 128), F32)],
        8,
        "v_part",
    )(z, factor)
    v = lax.all_to_all(v, "gy", 0, 0, tiled=True)
    v = call(
        sum_kernel,
        ((16, 16 * count + tail, 128), BF16),
        [VMEM],
        [pltpu.VMEM((16 * count, 128), F32), pltpu.VMEM((16, tail, 128), F32)],
        8,
        "v_sum_plane",
    )(v)
    v = lax.all_to_all(v, "gx", 0, 0, tiled=True)
    return call(
        functools.partial(rows_kernel, count),
        ((32, 4, 128), F32),
        [SMEM, VMEM],
        [pltpu.VMEM((16 * count + tail, 128), F32)],
        8,
        "v_rows",
    )(idx, v)


def local(moment, factor):
    plane = ("gy", "gz")
    idx = (2 * lax.axis_index("gx") + lax.axis_index("gz")).astype(jnp.int32).reshape(1)
    first_core = lax.rem(idx[0], 2) == 0
    there, ut = y_there(idx, first_core.astype(jnp.int32).reshape(1), moment, factor)
    came = lax.ppermute(there, "gz", [(0, 1), (1, 0)])
    here = y_here(idx, moment, ut)
    y = (here.astype(F32) + came.astype(F32)).astype(BF16)
    y = lax.all_to_all(y, "gy", 0, 0, tiled=True)
    z = call(
        z_kernel,
        ((16, 16, 128), BF16),
        [VMEM, VMEM],
        [pltpu.VMEM((2, 128, 128), F32)],
        8,
        "z_block",
    )(y, factor)
    z = lax.all_to_all(z, "gx", 0, 0, tiled=True)
    z = lax.all_gather(z, "gz", axis=0, tiled=True)
    branches = [functools.partial(v_share, share) for share in SHARES]
    v = lax.cond(first_core, *branches, idx, z.reshape(512, 128), factor)
    v = lax.all_to_all(v, plane, 0, 0, tiled=True)
    return call(final_kernel, ((64, 128), F32), [VMEM], [], 8, "scaled")(v.reshape(128, 128))


def solution(mesh):
    in_specs = (P("gx", "gy", "gz"), P())
    out_specs = P("gx", None)
    return jax.shard_map(local, mesh=mesh, in_specs=in_specs, out_specs=out_specs, check_vma=False)
```

```python
import functools

import jax
import jax.numpy as jnp
from jax import lax
from jax.experimental import pallas as pl
from jax.experimental.pallas import tpu as pltpu
from jax.sharding import PartitionSpec as P

F32 = jnp.float32
BF16 = jnp.bfloat16
MIB = 1 << 20
VMEM = pl.BlockSpec(memory_space=pltpu.VMEM)
ANY = pl.BlockSpec(memory_space=pl.ANY)
SMEM = pl.BlockSpec(memory_space=pltpu.SMEM)


def params(mib):
    return pltpu.CompilerParams(vmem_limit_bytes=mib * MIB)


def y_store(ut, rows, first, out_ref):
    y = lax.dot_general(ut, rows, (((1,), (1,)), ((), ())), preferred_element_type=F32)
    parts = [y[:, n : n + 128].reshape(16, 8, 128) for n in range(0, y.shape[1], 128)]
    out_ref[:, 8 * first : 8 * (first + len(parts)), :] = jnp.concatenate(parts, axis=1).astype(BF16)


CHUNK = 8
CHUNKS = 16 // CHUNK
DOT = 2
HALF = (CHUNKS, 2, CHUNK, 64, 512)


def y_copies(half, m_ref, buf, sem):
    copies = []
    for t in range(CHUNKS):
        for h in range(2):
            block = m_ref.at[pl.ds(32 * half + 16 * h + CHUNK * t, CHUNK)]
            copies.append(pltpu.make_async_copy(block, buf.at[t, h], sem.at[t, h]))
            copies[-1].start()
    return copies


def y_chunk(t, ut, buf, out_ref):
    for p in range(0, CHUNK, DOT):
        rows = jnp.concatenate([buf[t, h, p + n] for n in range(DOT) for h in range(2)], axis=0)
        y_store(ut, rows, CHUNK * t + p, out_ref)


def stage_kernel(first_core_ref, m_ref, theirs_ref, sem):
    for copy in y_copies(first_core_ref[0], m_ref, theirs_ref, sem):
        copy.wait()


def y_there_kernel(idx_ref, theirs_ref, u_ref, out_ref, ut_ref):
    core = lax.rem(idx_ref[0], 2)
    ut_ref[...] = u_ref[pl.ds(pl.multiple_of(512 * core, 512), 512), :].T
    for t in range(CHUNKS):
        y_chunk(t, ut_ref[...], theirs_ref, out_ref)


def y_here_kernel(idx_ref, m_ref, ut_ref, out_ref, buf, sem):
    copies = y_copies(lax.rem(idx_ref[0], 2), m_ref, buf, sem)
    for t in range(CHUNKS):
        copies[2 * t].wait()
        copies[2 * t + 1].wait()
        y_chunk(t, ut_ref[...], buf, out_ref)


def y_there(idx, first_core, moment, factor):
    theirs = pl.pallas_call(
        stage_kernel,
        out_shape=jax.ShapeDtypeStruct(HALF, BF16),
        in_specs=[SMEM, ANY],
        out_specs=VMEM,
        scratch_shapes=[pltpu.SemaphoreType.DMA((CHUNKS, 2))],
        compiler_params=params(48),
        name="stage",
    )(first_core, moment)
    return pl.pallas_call(
        y_there_kernel,
        out_shape=[jax.ShapeDtypeStruct((16, 128, 128), BF16), jax.ShapeDtypeStruct((128, 512), BF16)],
        in_specs=[SMEM, VMEM, VMEM],
        out_specs=[VMEM, VMEM],
        compiler_params=params(48),
        name="y_there",
    )(idx, theirs, factor)


def y_here(idx, moment, ut):
    return pl.pallas_call(
        y_here_kernel,
        out_shape=jax.ShapeDtypeStruct((16, 128, 128), BF16),
        in_specs=[SMEM, ANY, VMEM],
        out_specs=VMEM,
        scratch_shapes=[pltpu.VMEM(HALF, BF16), pltpu.SemaphoreType.DMA((CHUNKS, 2))],
        compiler_params=params(48),
        name="y_here",
    )(idx, moment, ut)


def z_kernel(y_ref, u_ref, out_ref, z_ref):
    lhs = []
    for i2 in range(2):
        cut = [y_ref[s][:, 64 * i2 : 64 * i2 + 64] for s in range(16)]
        lhs.append(jnp.concatenate(cut, axis=1))
    z = jnp.dot(jnp.concatenate(lhs, axis=0), u_ref[...], preferred_element_type=F32) * (1.0 / 32.0)
    z_ref[0] = z[0:128]
    z_ref[1] = z[128:256]
    for b in range(8):
        low, high = [z_ref[i2, pl.ds(b, 16, stride=8), :] for i2 in range(2)]
        out_ref[2 * b] = jnp.concatenate([low[:, 0:64], high[:, 0:64]], axis=1).astype(BF16)
        out_ref[2 * b + 1] = jnp.concatenate([low[:, 64:128], high[:, 64:128]], axis=1).astype(BF16)


SHARES = (((0, 0),), ((0, 1), (1, 0), (1, 1)))


def v_kernel(share, z_ref, u_ref, out_ref, w_ref, v_ref):
    u = u_ref[...].reshape(16, 4, 16, 128)
    uw = [jnp.concatenate([u[:, 2 * h + i2].reshape(256, 128) for h in range(2)], axis=0) for i2 in range(2)]
    uw = jnp.concatenate(uw, axis=1)
    full = lax.dot_general(z_ref[...], uw, (((0,), (0,)), ((), ())), preferred_element_type=F32)
    c = ((full[0:64, 0:128] + full[64:128, 128:256]) * (1.0 / 32.0)).astype(BF16)
    w_ref[...] = jnp.zeros(w_ref.shape, BF16)
    w_ref[0, 0:64] = c
    w_ref[1, 64:128] = c
    for n, (half, i2) in enumerate(share):
        rows = z_ref[256 * half : 256 * half + 256, :]
        v_ref[n] = jnp.dot(rows, w_ref[i2], preferred_element_type=F32)
        for ip in range(16):
            out_ref[ip, 16 * n : 16 * n + 16, :] = v_ref[n, pl.ds(ip, 16, stride=16), :]


def sum_kernel(in_ref, out_ref, mid_ref, tail_ref):
    total = jnp.sum(in_ref[...], axis=0) * (1.0 / 128.0)
    count = total.shape[0] // 16
    high = total.astype(BF16).astype(F32)
    rest = total - high
    mid_ref[...] = rest
    tail_ref[...] = jnp.zeros(tail_ref.shape, F32)
    for n in range(count):
        group = high[16 * n : 16 * n + 16]
        size = jnp.sum(group * group, axis=0, keepdims=True)
        error = jnp.sum(group * rest[16 * n : 16 * n + 16], axis=0, keepdims=True)
        ratio = jnp.where(size > 0.0, error / jnp.where(size > 0.0, size, 1.0), 0.0)
        ratio = jnp.clip(ratio, -(2.0**-8), 2.0**-8)
        for d in range(16):
            tail_ref[d, n : n + 1, :] = ratio
            tail_ref[d, count + n : count + n + 1, :] = mid_ref[16 * n + d : 16 * n + d + 1, :]
    high = jnp.broadcast_to(high[None], (16,) + high.shape)
    out_ref[...] = jnp.concatenate([high, tail_ref[...]], axis=1).astype(BF16)


def rows_kernel(count, idx_ref, in_ref, out_ref, v_ref):
    parts = in_ref[...].astype(F32)
    v = jnp.sum(parts, axis=0)
    v_ref[...] = v
    first = 16 * count
    squares = jnp.zeros((16, 128), F32)
    for n in range(count):
        group = parts[:, 16 * n : 16 * n + 16]
        rows = v[16 * n : 16 * n + 16] + jnp.sum(group * parts[:, first + n : first + n + 1], axis=0)
        squares = squares + rows * rows
    squares = jnp.sum(squares, axis=0, keepdims=True)
    block = idx_ref[0] // 2
    own = jnp.concatenate([v_ref[pl.ds(16 * n + block, 1), :] for n in range(count)], axis=0)
    own = own + v[first + count : first + 2 * count]
    own = [own] if count == 3 else [own, jnp.zeros((3 - count, 128), F32)]
    message = jnp.concatenate(own + [squares], axis=0)
    out_ref[...] = jnp.broadcast_to(message[None], out_ref.shape)


def final_kernel(in_ref, out_ref):
    total = jnp.sum(in_ref[pl.ds(3, 32, stride=4), :], axis=0, keepdims=True)
    total = jnp.sum(total, axis=1, keepdims=True)
    scale = lax.rsqrt(total / (1024 * 128) + 1e-06)
    for core, share in enumerate(SHARES):
        for n, (half, i2) in enumerate(share):
            first = 32 * half + 16 * i2
            out_ref[first : first + 16, :] = in_ref[pl.ds(4 * core + n, 16, stride=8), :] * scale


def call(kernel, out, specs, scratch, mib, name):
    return pl.pallas_call(
        kernel,
        out_shape=jax.ShapeDtypeStruct(*out),
        in_specs=specs,
        out_specs=VMEM,
        scratch_shapes=scratch,
        compiler_params=params(mib),
        name=name,
    )


def v_share(share, idx, z, factor):
    count = len(share)
    tail = -(-2 * count // 8) * 8
    v = call(
        functools.partial(v_kernel, share),
        ((16, 16 * count, 128), F32),
        [VMEM, VMEM],
        [pltpu.VMEM((2, 128, 128), BF16), pltpu.VMEM((count, 256, 128), F32)],
        8,
        "v_part",
    )(z, factor)
    v = lax.all_to_all(v, "gy", 0, 0, tiled=True)
    v = call(
        sum_kernel,
        ((16, 16 * count + tail, 128), BF16),
        [VMEM],
        [pltpu.VMEM((16 * count, 128), F32), pltpu.VMEM((16, tail, 128), F32)],
        8,
        "v_sum_plane",
    )(v)
    v = lax.all_to_all(v, "gx", 0, 0, tiled=True)
    return call(
        functools.partial(rows_kernel, count),
        ((32, 4, 128), F32),
        [SMEM, VMEM],
        [pltpu.VMEM((16 * count + tail, 128), F32)],
        8,
        "v_rows",
    )(idx, v)


def local(moment, factor):
    plane = ("gy", "gz")
    idx = (2 * lax.axis_index("gx") + lax.axis_index("gz")).astype(jnp.int32).reshape(1)
    first_core = lax.rem(idx[0], 2) == 0
    there, ut = y_there(idx, first_core.astype(jnp.int32).reshape(1), moment, factor)
    came = lax.ppermute(there, "gz", [(0, 1), (1, 0)])
    here = y_here(idx, moment, ut)
    y = (here.astype(F32) + came.astype(F32)).astype(BF16)
    y = lax.all_to_all(y, "gy", 0, 0, tiled=True)
    z = call(
        z_kernel,
        ((16, 16, 128), BF16),
        [VMEM, VMEM],
        [pltpu.VMEM((2, 128, 128), F32)],
        8,
        "z_block",
    )(y, factor)
    z = lax.all_to_all(z, "gx", 0, 0, tiled=True)
    z = lax.all_gather(z, "gz", axis=0, tiled=True)
    branches = [functools.partial(v_share, share) for share in SHARES]
    v = lax.cond(first_core, *branches, idx, z.reshape(512, 128), factor)
    v = lax.all_to_all(v, plane, 0, 0, tiled=True)
    return call(final_kernel, ((64, 128), F32), [VMEM], [], 8, "scaled")(v.reshape(128, 128))


def solution(mesh):
    in_specs = (P("gx", "gy", "gz"), P())
    out_specs = P("gx", None)
    return jax.shard_map(local, mesh=mesh, in_specs=in_specs, out_specs=out_specs, check_vma=False)
```
